32 devices in a mesh: col: 4 (over x, core), grp: 8 (over z, y).
Axes of the slice: x: 2, y: 2, z: 4, core: 2. Of those that a mesh axis runs over, the one named last changes fastest.
Arguments:
- grid_fields: bfloat16 [1024, 512], P(('col', 'grp')), may hold values from -6 to 6
- brick_slot: int32 [1024], P('col'), may hold values from 0 to 255, as said below
- block_brick: int32 [1024], P(('col', 'grp')), may hold values from 0 to 287, as said below
- node_mask: int32 [1024, 64], P(('col', 'grp')), may hold values 0 or 1
- counts: int32 [1024], P(('col', 'grp')), may hold values from 1 to 128, as said below
- shape_t: bfloat16 [1024, 64, 128], P(('col', 'grp')), may hold values from 0 to 0.099609375
- part_mass: float32 [1024, 128], P(('col', 'grp')), may hold values from 0.5 to 2
- part_vel: float32 [1024, 3, 128], P(('col', 'grp')), may hold values from -6 to 6
Outputs:
- vel_new: float32 [1024, 3, 128], P(('col', 'grp'))
- grid_momentum: float32 [1024, 256], P(('col', 'grp'))
The draws below stay inside these ranges and needn't reach their ends.
Inputs may be any that keep to these rules, and one draw needn't show every extreme that they name: `brick_slot`: each aligned run of 256 entries is a permutation of 0 .. 255. `block_brick`: the first block of each device refers to a left neighbour brick, the second to a right neighbour brick, all others to bricks of the column itself; of one device's blocks at most 4 refer to bricks stored on any one device of the column, and exactly 4 to some device. `counts`: the first block of each device is full.
All inputs are finite; a program needn't handle non-finite values. No bound on the sum of `node_mask` on one device may be relied on, other than what follows from the above.
Results may differ from the reference program's by a relative error of at most 0.00041.
Values may be sent and summed in bfloat16 or wider, within the bound.
A program may use at most 64 MiB of HBM per device.

```python
import math
import jax
import jax.numpy as jnp
from jax import lax

NODES = 64
FIELDS = 8
OUTF = 4
PBLK = 128
RIM = 16
BRICK_DEV = 32
BLK_DEV = 32
CAP = 4
BC = 256
NBRICKS = 1024
BLK_COL = 256
NBLOCKS = 1024


def slot_orders(key):
    keys = jax.random.split(jax.random.fold_in(key, 5), NBRICKS // BC)
    return jax.vmap(lambda one_key: jax.random.permutation(one_key, BC))(keys).astype(jnp.int32)


def draw_brick_slot(key, part):
    return slot_orders(key).reshape(-1).astype(jnp.int32)


def draw_block_brick(key, part):
    orders = slot_orders(key)
    groups = BC // BRICK_DEV
    devices = NBLOCKS // BLK_DEV
    inverse = jnp.argsort(orders, axis=1).astype(jnp.int32)
    owner_keys = jax.random.split(jax.random.fold_in(key, 14), devices)
    owner_perm = jax.vmap(lambda one_key: jax.random.permutation(one_key, groups))(owner_keys).astype(jnp.int32)
    within = jnp.arange(BLK_DEV, dtype=jnp.int32)
    pick = jnp.maximum(within - 2, 0) // CAP % groups
    owners = owner_perm[:, pick]
    rows = jax.random.randint(jax.random.fold_in(key, 15), (devices, BLK_DEV), 0, BRICK_DEV).astype(jnp.int32)
    storage = owners * BRICK_DEV + rows
    column_of = (jnp.arange(devices, dtype=jnp.int32) // groups)[:, None]
    own = inverse[column_of, storage] + RIM
    left = jax.random.randint(jax.random.fold_in(key, 12), (devices, BLK_DEV), 0, RIM).astype(jnp.int32)
    right = jax.random.randint(jax.random.fold_in(key, 13), (devices, BLK_DEV), BC + RIM, BC + 2 * RIM).astype(jnp.int32)
    mixed = jnp.where(within[None, :] == 0, left, jnp.where(within[None, :] == 1, right, own))
    return mixed.reshape(-1).astype(jnp.int32)


def draw_counts(key, part):
    base = jax.random.randint(jax.random.fold_in(key, 21), (NBLOCKS,), 1, PBLK + 1)
    within = jnp.arange(NBLOCKS, dtype=jnp.int32) % BLK_DEV
    return jnp.where(within == 0, PBLK, base).astype(jnp.int32)


def with_ends(entries, stream_key, low, largest):
    spot = [jax.random.randint(jax.random.fold_in(stream_key, axis), (), 0, length) for axis, length in enumerate(entries.shape)]
    main_axis = entries.shape.index(max(entries.shape))
    neighbour = spot[:main_axis] + [(spot[main_axis] + 1) % entries.shape[main_axis]] + spot[main_axis + 1:]
    return entries.at[tuple(spot)].set(low).at[tuple(neighbour)].set(largest)


def block_scale(rng, shape, cuts, smallest, top_value):
    def one(position, blocks):
        heights = jax.random.uniform(jax.random.fold_in(jax.random.fold_in(rng, 6), position), (blocks,), jnp.float32, smallest / len(cuts), top_value / len(cuts))
        return jnp.repeat(jnp.exp(heights), shape[position] // blocks).reshape((-1,) + (1,) * (len(shape) - position - 1))

    level = one(*cuts[0])
    for cut in cuts[1:]:
        level = level * one(*cut)
    return level


def scatter_about(own_key, extent, spread, limit, cuts=(), kind=jnp.bfloat16):
    array = jax.random.normal(own_key, extent, jnp.float32) * spread
    if len(cuts) > 0:
        array = block_scale(own_key, extent, cuts, -0.22, 0.18) * array
    return jnp.clip(array, min=-limit, max=limit).astype(kind)


def setup_inputs(seed: int = 0) -> dict:
    splits = jax.random.split(jax.random.key(seed), 9)
    return {
        "grid_fields": scatter_about(splits[0], (NBRICKS, FIELDS * NODES), 1.0, 6.0, ((0, 32),)),
        "brick_slot": draw_brick_slot(jax.random.fold_in(splits[8], 71), 0),
        "block_brick": draw_block_brick(jax.random.fold_in(splits[8], 71), 0),
        "node_mask": with_ends((jax.random.randint(splits[3], (NBLOCKS, NODES), 0, 4) < 3).astype(jnp.int32), jax.random.fold_in(splits[3], 1), 0, 1),
        "counts": draw_counts(jax.random.fold_in(splits[8], 71), 0),
        "shape_t": jnp.clip(0.099609375 * jax.random.uniform(splits[5], (NBLOCKS, NODES, PBLK), jnp.float32) ** block_scale(splits[5], (NBLOCKS, NODES, PBLK), ((0, 32),), -0.2, 0.2), 0.0, 0.099609375).astype(jnp.bfloat16),
        "part_mass": jnp.clip(jnp.exp(math.log(2.0) - 1.3862944 * jax.random.uniform(splits[6], (NBLOCKS, PBLK), jnp.float32) ** block_scale(splits[6], (NBLOCKS, PBLK), ((0, 32),), -0.2, 0.2)), 0.5, 2.0),
        "part_vel": scatter_about(splits[7], (NBLOCKS, 3, PBLK), 1.0, 6.0, ((0, 32),), jnp.float32),
    }


def column_work(items):
    ext_col, bricks, mask, count, shapes, mass, vel = items
    rows = jnp.take(ext_col, bricks, axis=0).reshape(-1, FIELDS, NODES)
    weights = shapes * mask[:, :, None].astype(jnp.bfloat16)
    interp = jnp.einsum("bfn,bnp->bfp", rows.astype(jnp.float32), weights.astype(jnp.float32))
    live = (jnp.arange(PBLK, dtype=jnp.int32)[None, :] < count[:, None]).astype(jnp.float32)
    blend = 0.4 * interp[:, 0:3] + 0.6 * (vel + interp[:, 3:6])
    vel_next = blend / (1.0 + 0.5 * interp[:, 7:8] * interp[:, 7:8]) * live[:, None, :]
    first = mass * (1.0 + 0.5 * jnp.tanh(interp[:, 6])) * live
    contrib = jnp.concatenate([first[:, None, :], mass[:, None, :] * vel_next], axis=1).astype(jnp.bfloat16)
    partial_value = jnp.einsum("bfp,bnp->bfn", contrib.astype(jnp.float32), weights.astype(jnp.float32))
    partial_value = partial_value.reshape(-1, OUTF * NODES)
    summed = jax.ops.segment_sum(partial_value, bricks, num_segments=BC + 2 * RIM)
    return vel_next, summed


def reference(grid_fields, brick_slot, block_brick, node_mask, counts, shape_t, part_mass, part_vel):
    ncols = NBRICKS // BC
    stored = grid_fields.reshape(ncols, BC, FIELDS * NODES)
    slots = brick_slot.reshape(ncols, BC)
    logical = jnp.take_along_axis(stored, slots[:, :, None], axis=1)
    zero_rows = jnp.zeros((1, RIM, FIELDS * NODES), jnp.bfloat16)
    left = jnp.concatenate([zero_rows, logical[:-1, BC - RIM:]], axis=0)
    right = jnp.concatenate([logical[1:, :RIM], zero_rows], axis=0)
    extended = jnp.concatenate([left, logical, right], axis=1)
    blocks = BLK_COL
    items = (extended,
             block_brick.reshape(ncols, blocks),
             node_mask.reshape(ncols, blocks, NODES),
             counts.reshape(ncols, blocks),
             shape_t.reshape(ncols, blocks, NODES, PBLK),
             part_mass.reshape(ncols, blocks, PBLK),
             part_vel.reshape(ncols, blocks, 3, PBLK))
    vel_next, summed = lax.map(column_work, items)
    middle = summed[:, RIM:RIM + BC]
    zero_sum = jnp.zeros((1, RIM, OUTF * NODES), summed.dtype)
    from_left = jnp.concatenate([zero_sum, summed[:-1, RIM + BC:]], axis=0)
    from_right = jnp.concatenate([summed[1:, :RIM], zero_sum], axis=0)
    middle = middle.at[:, :RIM].add(from_left)
    middle = middle.at[:, BC - RIM:].add(from_right)
    column_ids = jnp.arange(ncols, dtype=jnp.int32)[:, None]
    storage = jnp.zeros_like(middle).at[column_ids, slots].set(middle)
    return vel_next.reshape(NBLOCKS, 3, PBLK), storage.reshape(NBRICKS, OUTF * NODES)
```

```python
import functools

import jax
import jax.numpy as jnp
from jax import lax
from jax.experimental import pallas as pl
from jax.experimental.pallas import tpu as pltpu
from jax.sharding import PartitionSpec as P

NODES = 64
FIELDS = 8
OUTF = 4
PBLK = 128
RIM = 16
LANES = 128
PIECES = 4
MESH = pl.DeviceIdType.MESH
F32 = jnp.float32
BF16 = jnp.bfloat16


def iota(shape, dim):
    return lax.broadcasted_iota(jnp.int32, shape, dim)


def kernel(
    ncols, groups, slots,
    bb_ref, slot_ref, cnt_ref, grid_in, mask_in, mass_in, w_in, pv_in,
    vel_ref, mom_ref,
    grid_v, mask_v, mass_v, w_v, pv_v,
    req_out, edge_out, req_in, f_out, f_in, p_out, p_in,
    in_sem, self_sem, send_sem, recv_sem,
):
    blocks = bb_ref.shape[1]
    columns = slot_ref.shape[1]
    rows = grid_in.shape[0]
    width = groups * PIECES * slots
    c = lax.axis_index("col")
    g = lax.axis_index("grp")
    has = (c > 0, None, c < ncols - 1)

    barrier = pltpu.get_barrier_semaphore()

    def peers(body_own, body_left, body_right):
        def own(i, carry):
            body_own(lax.rem(g + i, groups))
            return carry

        def side(body):
            def run(i, carry):
                body(lax.rem(g + i, groups))
                return carry
            lax.fori_loop(0, groups, run, 0, unroll=groups <= 8)

        pl.when(has[0])(lambda: side(body_left))
        pl.when(has[2])(lambda: side(body_right))
        lax.fori_loop(1, groups, own, 0, unroll=groups <= 8)

    def greet(dc):
        def go(d):
            pl.semaphore_signal(barrier, inc=1, device_id=(c + dc, d), device_id_type=MESH)
        return go

    peers(greet(0), greet(-1), greet(1))
    loads = [
        pltpu.make_async_copy(src, dst, in_sem.at[i])
        for i, (src, dst) in enumerate(
            ((grid_in, grid_v), (mask_in, mask_v), (mass_in, mass_v), (pv_in, pv_v), (w_in, w_v))
        )
    ]
    for load in loads:
        load.start()

    bb = bb_ref[...].astype(F32)
    slotf = slot_ref[...].astype(F32)
    eye = iota((blocks, blocks), 0) == iota((blocks, blocks), 1)

    def to_col(row):
        return jnp.sum(jnp.where(eye, row, 0.0), axis=1, keepdims=True)

    bb_col = to_col(bb)
    own_col = bb_col.astype(jnp.int32) - RIM
    is_own = (own_col >= 0) & (own_col < columns)
    hit = iota((blocks, columns), 1) == own_col
    slot_col = jnp.sum(jnp.where(hit, slotf, 0.0), axis=1, keepdims=True).astype(jnp.int32)
    owner = jnp.where(is_own, lax.div(slot_col, rows), -1)
    row_at = slot_col - owner * rows
    owner_row = jnp.sum(jnp.where(eye, owner.astype(F32), 0.0), axis=0, keepdims=True)
    same = (owner_row == owner.astype(F32)) & (iota((blocks, blocks), 1) < iota((blocks, blocks), 0))
    rank = jnp.sum(jnp.where(same, 1.0, 0.0), axis=1, keepdims=True).astype(jnp.int32)
    dest = jnp.where(is_own, owner * slots + rank, -1)
    ask = jnp.where(is_own, row_at + 1, 0).astype(F32)

    lane = iota((1, width), 1)
    lane_r = lane & (slots - 1)
    lane_j = lax.div(lane, slots) & (PIECES - 1)
    lane_g = lax.div(lane, slots * PIECES)
    from_me = lane_g == g

    def write_request(d, carry):
        match = dest == d * slots + lane_r
        values = jnp.sum(jnp.where(match, ask, 0.0), axis=0, keepdims=True)
        req_out[d] = jnp.where(from_me, values, 0.0)
        return carry

    lax.fori_loop(0, groups, write_request, 0, unroll=groups <= 8)
    first = from_me & (lane_r == 0)
    edge_out[0] = jnp.where(first, bb[:, 0:1] + 1.0, 0.0)
    edge_out[1] = jnp.where(first, bb[:, 1:2] - (columns + RIM) + 1.0, 0.0)

    def exchange(phase, out_of, into):
        def send(sec):
            def go(d):
                pltpu.make_async_remote_copy(
                    src_ref=out_of(sec, d),
                    dst_ref=into.at[(2 - sec) * groups + g],
                    send_sem=send_sem.at[phase, sec],
                    recv_sem=recv_sem.at[phase, 2 - sec],
                    device_id=(c + sec - 1, d),
                    device_id_type=MESH,
                ).start()
            return go

        peers(send(1), send(0), send(2))
        pltpu.make_async_copy(out_of(1, g), into.at[groups + g], self_sem.at[phase]).start()

    def bytes_wait(ref, start, count, sem):
        part = ref.at[pl.ds(start, count)]
        pltpu.make_async_copy(part, part, sem).wait()

    def arrive(phase, into):
        bytes_wait(into, groups, 1, self_sem.at[phase])
        bytes_wait(into, groups, groups - 1, recv_sem.at[phase, 1])
        for sec in (0, 2):
            pl.when(has[sec])(
                lambda sec=sec: bytes_wait(into, sec * groups, groups, recv_sem.at[phase, sec])
            )

    def sent(phase, into):
        bytes_wait(into, groups, groups - 1, send_sem.at[phase, 1])
        for sec in (0, 2):
            pl.when(has[sec])(
                lambda sec=sec: bytes_wait(into, sec * groups, groups, send_sem.at[phase, sec])
            )

    def clear(sec):
        for ref in (req_in, f_in, p_in):
            part = ref.at[pl.ds(sec * groups, groups)]
            part[...] = jnp.zeros(part.shape, ref.dtype)

    for sec in (0, 2):
        pl.when(jnp.logical_not(has[sec]))(lambda sec=sec: clear(sec))

    count = groups - 1 + jnp.where(has[0], groups, 0) + jnp.where(has[2], groups, 0)
    pl.semaphore_wait(barrier, count)
    exchange(
        0,
        lambda sec, d: req_out.at[d] if sec == 1 else edge_out.at[sec // 2],
        req_in,
    )

    ls = lane_g * slots + lane_r
    mine = jnp.where(dest == ls, 1.0, 0.0)
    zero_slot = lane_r == 0
    sub = iota((blocks, width), 0)
    from_left = jnp.where((sub == 0) & zero_slot, 1.0, 0.0)
    from_right = jnp.where((sub == 1) & zero_slot, 1.0, 0.0)
    wide = jnp.concatenate([from_left, mine, from_right], axis=1)
    wide_j = jnp.concatenate([lane_j] * 3, axis=1)
    unpack = jnp.concatenate(
        [jnp.where(wide_j == j, wide, 0.0) for j in range(PIECES)], axis=0
    ).astype(BF16)

    edge_lane = iota((RIM, columns), 1)
    edge_sub = iota((RIM, columns), 0)
    edge_low = jnp.sum(jnp.where(edge_lane == edge_sub, slotf, 0.0), axis=1, keepdims=True)
    edge_high = jnp.sum(
        jnp.where(edge_lane == edge_sub + (columns - RIM), slotf, 0.0), axis=1, keepdims=True
    )
    cnt_col = to_col(cnt_ref[...].astype(F32))
    loads[0].wait()
    grid = grid_v[...]
    grid_stack = jnp.concatenate(
        [grid[:, j * LANES : (j + 1) * LANES] for j in range(PIECES)], axis=0
    )
    loads[1].wait()
    mask = mask_v[...].astype(F32)
    mask2 = jnp.concatenate([mask, mask], axis=1)
    half = iota((1, LANES), 1) >= NODES
    low = jnp.logical_not(half)

    arrive(0, req_in)

    def asked(sec):
        total = req_in[sec * groups]
        for i in range(1, groups):
            total = total + req_in[sec * groups + i]
        return total - 1.0

    def edge_rows(value, table):
        match = iota((RIM, width), 0).astype(F32) == value
        found = jnp.sum(jnp.where(match, table + 1.0, 0.0), axis=0, keepdims=True)
        return found - 1.0 - (g * rows).astype(F32)

    want = jnp.concatenate(
        [edge_rows(asked(0), edge_low), asked(1), edge_rows(asked(2), edge_high)], axis=1
    )
    give = jnp.where(iota((rows, 3 * width), 0).astype(F32) == want, 1.0, 0.0)
    pieces = [jnp.where(wide_j == j, give, 0.0) for j in range(PIECES)]
    pack = jnp.concatenate(pieces, axis=0).astype(BF16)

    def across(matrix, stack):
        return lax.dot_general(
            matrix, stack, (((0,), (0,)), ((), ())), preferred_element_type=F32
        ).astype(BF16).reshape(3 * groups, PIECES * slots, LANES)

    f_out[...] = across(pack, grid_stack)
    exchange(1, lambda sec, d: f_out.at[sec * groups + d], f_in)

    place = [
        (pieces[t] + pieces[t + 2]).astype(BF16) for t in range(2)
    ]
    loads[2].wait()
    loads[3].wait()
    loads[4].wait()
    arrive(1, f_in)

    fields = jnp.dot(
        unpack, f_in[...].reshape(3 * width, LANES), preferred_element_type=F32
    )
    tiles = []
    for j in range(PIECES):
        v = fields[j * blocks : (j + 1) * blocks]
        r = pltpu.roll(v, NODES, 1)
        tiles.append(jnp.where(low, v, r) * mask2)
        tiles.append(jnp.where(low, r, v) * mask2)

    step = 8
    local = iota((step, LANES), 0)
    diag = [local == 2 * t + half.astype(jnp.int32) for t in range(step // 2)]
    sums = [[], []]
    plane = iota((step, PBLK), 1).astype(F32)
    for s in range(blocks // step):
        at = slice(s * step, (s + 1) * step)
        lhs = jnp.concatenate(
            [
                jnp.concatenate([jnp.where(d, tile[at], 0.0) for d in diag], axis=1)
                for tile in tiles
            ],
            axis=0,
        ).astype(BF16)
        w = w_v[pl.ds(s * step * NODES, step * NODES), :]
        interp = jnp.dot(lhs, w, preferred_element_type=F32)
        f = [interp[i * step : (i + 1) * step] for i in range(FIELDS)]
        live = jnp.where(plane < cnt_col[at], 1.0, 0.0)
        mass = mass_v[at, :]
        scale = live / (1.0 + 0.5 * f[7] * f[7])
        contrib = [mass * (1.0 + 0.5 * jnp.tanh(f[6])) * live]
        for k in range(3):
            vel = (0.4 * f[k] + 0.6 * (pv_v[k, at, :] + f[3 + k])) * scale
            vel_ref[k, at, :] = vel
            contrib.append(mass * vel)
        back = lax.dot_general(
            jnp.concatenate(contrib, axis=0).astype(BF16),
            w,
            (((1,), (1,)), ((), ())),
            preferred_element_type=F32,
        )
        folded = []
        for k in range(OUTF):
            o = back[k * step : (k + 1) * step]
            a = jnp.where(diag[0], o[:, :LANES], 0.0)
            for t in range(1, step // 2):
                a = a + jnp.where(diag[t], o[:, t * LANES : (t + 1) * LANES], 0.0)
            folded.append(a + pltpu.roll(a, NODES, 1))
        for t in range(2):
            sums[t].append(jnp.where(low, folded[2 * t], folded[2 * t + 1]) * mask2[at])

    partial = [jnp.concatenate(x, axis=0) for x in sums]
    high = [x.astype(BF16) for x in partial]
    rest = [(x - h.astype(F32)).astype(BF16) for x, h in zip(partial, high)]
    p_out[...] = across(unpack, jnp.concatenate(high + rest, axis=0))
    exchange(2, lambda sec, d: p_out.at[sec * groups + d], p_in)
    sent(0, req_in)
    sent(1, f_in)
    arrive(2, p_in)
    arrived = p_in[...].reshape(3 * width, LANES)
    for t in range(2):
        mom_ref[:, t * LANES : (t + 1) * LANES] = jnp.dot(
            place[t], arrived, preferred_element_type=F32
        )
    sent(2, p_in)


def local(ncols, grid_fields, brick_slot, block_brick, node_mask, counts, shape_t, part_mass, part_vel):
    groups = lax.axis_size("grp")
    blocks = block_brick.shape[0]
    rows = grid_fields.shape[0]
    needed = max(2, (blocks - 2 + groups - 1) // groups)
    slots = 4
    while slots < needed:
        slots *= 2
    width = groups * PIECES * slots
    vmem = pl.BlockSpec(memory_space=pltpu.VMEM)
    hbm = pl.BlockSpec(memory_space=pl.ANY)
    message = (3 * groups, PIECES * slots, LANES)
    vel, momentum = pl.pallas_call(
        functools.partial(kernel, ncols, groups, slots),
        out_shape=(
            jax.ShapeDtypeStruct((3, blocks, PBLK), F32),
            jax.ShapeDtypeStruct((rows, OUTF * NODES), F32),
        ),
        in_specs=[vmem] * 3 + [hbm] * 5,
        out_specs=(vmem, vmem),
        scratch_shapes=[
            pltpu.VMEM(grid_fields.shape, BF16),
            pltpu.VMEM(node_mask.shape, jnp.int32),
            pltpu.VMEM(part_mass.shape, F32),
            pltpu.VMEM((blocks * NODES, PBLK), BF16),
            pltpu.VMEM((3, blocks, PBLK), F32),
            pltpu.VMEM((groups, 1, width), F32),
            pltpu.VMEM((2, 1, width), F32),
            pltpu.VMEM((3 * groups, 1, width), F32),
            pltpu.VMEM(message, BF16),
            pltpu.VMEM(message, BF16),
            pltpu.VMEM(message, BF16),
            pltpu.VMEM(message, BF16),
            pltpu.SemaphoreType.DMA((5,)),
            pltpu.SemaphoreType.DMA((3,)),
            pltpu.SemaphoreType.DMA((3, 3)),
            pltpu.SemaphoreType.DMA((3, 3)),
        ],
        compiler_params=pltpu.CompilerParams(
            collective_id=0, has_side_effects=True, vmem_limit_bytes=32 * 1024 * 1024
        ),
    )(
        block_brick.reshape(1, -1),
        brick_slot.reshape(1, -1),
        counts.reshape(1, -1),
        grid_fields,
        node_mask,
        part_mass,
        shape_t.reshape(blocks * NODES, PBLK),
        part_vel.transpose(1, 0, 2),
    )
    return vel.transpose(1, 0, 2), momentum


def solution(mesh):
    placed = (
        P(("col", "grp"), None),
        P("col"),
        P(("col", "grp")),
        P(("col", "grp"), None),
        P(("col", "grp")),
        P(("col", "grp"), None, None),
        P(("col", "grp"), None),
        P(("col", "grp"), None, None),
    )
    return jax.shard_map(
        functools.partial(local, mesh.shape["col"]),
        mesh=mesh,
        in_specs=placed,
        out_specs=(P(("col", "grp"), None, None), P(("col", "grp"), None)),
        check_vma=False,
    )
```

```python
import functools

import jax
import jax.numpy as jnp
from jax import lax
from jax.experimental import pallas as pl
from jax.experimental.pallas import tpu as pltpu
from jax.sharding import PartitionSpec as P

NODES = 64
FIELDS = 8
OUTF = 4
PBLK = 128
RIM = 16
LANES = 128
PIECES = 4
MESH = pl.DeviceIdType.MESH
F32 = jnp.float32
BF16 = jnp.bfloat16


def iota(shape, dim):
    return lax.broadcasted_iota(jnp.int32, shape, dim)


def kernel(
    ncols, groups, slots,
    bb_in, slot_in, cnt_in, grid_in, mask_in, mass_in, w_in, pv_in,
    vel_ref, place_ref, arrived_ref,
    bb_ref, slot_ref, cnt_ref, grid_v, mask_v, mass_v, w_v, pv_v,
    req_out, edge_out, req_in, f_out, f_in, p_out, p_in,
    in_sem, self_sem, send_sem, recv_sem,
):
    blocks = bb_ref.shape[1]
    columns = slot_ref.shape[1]
    rows = grid_in.shape[0]
    width = groups * PIECES * slots
    c = lax.axis_index("col")
    g = lax.axis_index("grp")
    has = (c > 0, None, c < ncols - 1)

    barrier = pltpu.get_barrier_semaphore()

    def peers(body_own, body_left, body_right):
        def own(i, carry):
            body_own(lax.rem(g + i, groups))
            return carry

        def side(body):
            def run(i, carry):
                body(lax.rem(g + i, groups))
                return carry
            lax.fori_loop(0, groups, run, 0, unroll=groups <= 8)

        pl.when(has[0])(lambda: side(body_left))
        pl.when(has[2])(lambda: side(body_right))
        lax.fori_loop(1, groups, own, 0, unroll=groups <= 8)

    def greet(dc):
        def go(d):
            pl.semaphore_signal(barrier, inc=1, device_id=(c + dc, d), device_id_type=MESH)
        return go

    loads = [
        pltpu.make_async_copy(src, dst, in_sem.at[i])
        for i, (src, dst) in enumerate(
            (
                (grid_in, grid_v), (mask_in, mask_v), (mass_in, mass_v), (pv_in, pv_v), (w_in, w_v),
                (bb_in, bb_ref), (slot_in, slot_ref), (cnt_in, cnt_ref),
            )
        )
    ]
    for i in (5, 6, 7, 0, 1, 4, 2, 3):
        loads[i].start()
    peers(greet(0), greet(-1), greet(1))
    loads[5].wait()
    loads[6].wait()

    bb = bb_ref[...].astype(F32)
    slotf = slot_ref[...].astype(F32)
    eye = iota((blocks, blocks), 0) == iota((blocks, blocks), 1)

    def to_col(row):
        return jnp.sum(jnp.where(eye, row, 0.0), axis=1, keepdims=True)

    bb_col = to_col(bb)
    own_col = bb_col.astype(jnp.int32) - RIM
    is_own = (own_col >= 0) & (own_col < columns)
    hit = iota((blocks, columns), 1) == own_col
    slot_col = jnp.sum(jnp.where(hit, slotf, 0.0), axis=1, keepdims=True).astype(jnp.int32)
    owner = jnp.where(is_own, lax.div(slot_col, rows), -1)
    row_at = slot_col - owner * rows
    owner_row = jnp.sum(jnp.where(eye, owner.astype(F32), 0.0), axis=0, keepdims=True)
    same = (owner_row == owner.astype(F32)) & (iota((blocks, blocks), 1) < iota((blocks, blocks), 0))
    rank = jnp.sum(jnp.where(same, 1.0, 0.0), axis=1, keepdims=True).astype(jnp.int32)
    dest = jnp.where(is_own, owner * slots + rank, -1)
    ask = jnp.where(is_own, row_at + 1, 0).astype(F32)

    lane = iota((1, width), 1)
    lane_r = lane & (slots - 1)
    lane_j = lax.div(lane, slots) & (PIECES - 1)
    lane_g = lax.div(lane, slots * PIECES)
    from_me = lane_g == g

    def write_request(d, carry):
        match = dest == d * slots + lane_r
        values = jnp.sum(jnp.where(match, ask, 0.0), axis=0, keepdims=True)
        req_out[d] = jnp.where(from_me, values, 0.0)
        return carry

    lax.fori_loop(0, groups, write_request, 0, unroll=groups <= 8)
    first = from_me & (lane_r == 0)
    edge_out[0] = jnp.where(first, bb[:, 0:1] + 1.0, 0.0)
    edge_out[1] = jnp.where(first, bb[:, 1:2] - (columns + RIM) + 1.0, 0.0)

    def exchange(phase, out_of, into):
        def send(sec):
            def go(d):
                pltpu.make_async_remote_copy(
                    src_ref=out_of(sec, d),
                    dst_ref=into.at[(2 - sec) * groups + g],
                    send_sem=send_sem.at[phase, sec],
                    recv_sem=recv_sem.at[phase, 2 - sec],
                    device_id=(c + sec - 1, d),
                    device_id_type=MESH,
                ).start()
            return go

        peers(send(1), send(0), send(2))
        pltpu.make_async_copy(out_of(1, g), into.at[groups + g], self_sem.at[phase]).start()

    def bytes_wait(ref, start, count, sem):
        part = ref.at[pl.ds(start, count)]
        pltpu.make_async_copy(part, part, sem).wait()

    def arrive(phase, into):
        bytes_wait(into, groups, 1, self_sem.at[phase])
        bytes_wait(into, groups, groups - 1, recv_sem.at[phase, 1])
        for sec in (0, 2):
            pl.when(has[sec])(
                lambda sec=sec: bytes_wait(into, sec * groups, groups, recv_sem.at[phase, sec])
            )

    def sent(phase, into):
        bytes_wait(into, groups, groups - 1, send_sem.at[phase, 1])
        for sec in (0, 2):
            pl.when(has[sec])(
                lambda sec=sec: bytes_wait(into, sec * groups, groups, send_sem.at[phase, sec])
            )

    def clear(sec):
        for ref in (req_in, f_in, p_in):
            part = ref.at[pl.ds(sec * groups, groups)]
            part[...] = jnp.zeros(part.shape, ref.dtype)

    for sec in (0, 2):
        pl.when(jnp.logical_not(has[sec]))(lambda sec=sec: clear(sec))

    count = groups - 1 + jnp.where(has[0], groups, 0) + jnp.where(has[2], groups, 0)
    pl.semaphore_wait(barrier, count)
    exchange(
        0,
        lambda sec, d: req_out.at[d] if sec == 1 else edge_out.at[sec // 2],
        req_in,
    )

    ls = lane_g * slots + lane_r
    mine = jnp.where(dest == ls, 1.0, 0.0)
    zero_slot = lane_r == 0
    sub = iota((blocks, width), 0)
    from_left = jnp.where((sub == 0) & zero_slot, 1.0, 0.0)
    from_right = jnp.where((sub == 1) & zero_slot, 1.0, 0.0)
    wide = jnp.concatenate([from_left, mine, from_right], axis=1)
    wide_j = jnp.concatenate([lane_j] * 3, axis=1)
    unpack = jnp.concatenate(
        [jnp.where(wide_j == j, wide, 0.0) for j in range(PIECES)], axis=0
    ).astype(BF16)

    edge_lane = iota((RIM, columns), 1)
    edge_sub = iota((RIM, columns), 0)
    edge_low = jnp.sum(jnp.where(edge_lane == edge_sub, slotf, 0.0), axis=1, keepdims=True)
    edge_high = jnp.sum(
        jnp.where(edge_lane == edge_sub + (columns - RIM), slotf, 0.0), axis=1, keepdims=True
    )
    loads[7].wait()
    cnt_col = to_col(cnt_ref[...].astype(F32))
    loads[0].wait()
    grid = grid_v[...]
    grid_stack = jnp.concatenate(
        [grid[:, j * LANES : (j + 1) * LANES] for j in range(PIECES)], axis=0
    )
    loads[1].wait()
    mask = mask_v[...].astype(F32)
    mask2 = jnp.concatenate([mask, mask], axis=1)
    half = iota((1, LANES), 1) >= NODES
    low = jnp.logical_not(half)

    arrive(0, req_in)

    def asked(sec):
        total = req_in[sec * groups]
        for i in range(1, groups):
            total = total + req_in[sec * groups + i]
        return total - 1.0

    def edge_rows(value, table):
        match = iota((RIM, width), 0).astype(F32) == value
        found = jnp.sum(jnp.where(match, table + 1.0, 0.0), axis=0, keepdims=True)
        return found - 1.0 - (g * rows).astype(F32)

    want = jnp.concatenate(
        [edge_rows(asked(0), edge_low), asked(1), edge_rows(asked(2), edge_high)], axis=1
    )
    give = jnp.where(iota((rows, 3 * width), 0).astype(F32) == want, 1.0, 0.0)
    pieces = [jnp.where(wide_j == j, give, 0.0) for j in range(PIECES)]
    pack = jnp.concatenate(pieces, axis=0).astype(BF16)

    def across(matrix, stack):
        return lax.dot_general(
            matrix, stack, (((0,), (0,)), ((), ())), preferred_element_type=F32
        ).astype(BF16).reshape(3 * groups, PIECES * slots, LANES)

    f_out[...] = across(pack, grid_stack)
    exchange(1, lambda sec, d: f_out.at[sec * groups + d], f_in)

    place_ref[...] = jnp.concatenate(
        [pieces[t] + pieces[t + 2] for t in range(2)], axis=0
    ).astype(BF16)
    loads[2].wait()
    loads[3].wait()
    loads[4].wait()
    arrive(1, f_in)

    fields = jnp.dot(
        unpack, f_in[...].reshape(3 * width, LANES), preferred_element_type=F32
    )
    tiles = []
    for j in range(PIECES):
        v = fields[j * blocks : (j + 1) * blocks]
        r = pltpu.roll(v, NODES, 1)
        tiles.append(jnp.where(low, v, r) * mask2)
        tiles.append(jnp.where(low, r, v) * mask2)

    step = 8
    local = iota((step, LANES), 0)
    diag = [local == 2 * t + half.astype(jnp.int32) for t in range(step // 2)]
    sums = [[], []]
    plane = iota((step, PBLK), 1).astype(F32)
    for s in range(blocks // step):
        at = slice(s * step, (s + 1) * step)
        lhs = jnp.concatenate(
            [
                jnp.concatenate([jnp.where(d, tile[at], 0.0) for d in diag], axis=1)
                for tile in tiles
            ],
            axis=0,
        ).astype(BF16)
        w = w_v[pl.ds(s * step * NODES, step * NODES), :]
        interp = jnp.dot(lhs, w, preferred_element_type=F32)
        f = [interp[i * step : (i + 1) * step] for i in range(FIELDS)]
        live = jnp.where(plane < cnt_col[at], 1.0, 0.0)
        mass = mass_v[at, :]
        scale = live / (1.0 + 0.5 * f[7] * f[7])
        contrib = [mass * (1.0 + 0.5 * jnp.tanh(f[6])) * live]
        for k in range(3):
            vel = (0.4 * f[k] + 0.6 * (pv_v[k, at, :] + f[3 + k])) * scale
            vel_ref[k, at, :] = vel
            contrib.append(mass * vel)
        back = lax.dot_general(
            jnp.concatenate(contrib, axis=0).astype(BF16),
            w,
            (((1,), (1,)), ((), ())),
            preferred_element_type=F32,
        )
        folded = []
        for k in range(OUTF):
            o = back[k * step : (k + 1) * step]
            a = jnp.where(diag[0], o[:, :LANES], 0.0)
            for t in range(1, step // 2):
                a = a + jnp.where(diag[t], o[:, t * LANES : (t + 1) * LANES], 0.0)
            folded.append(a + pltpu.roll(a, NODES, 1))
        for t in range(2):
            sums[t].append(jnp.where(low, folded[2 * t], folded[2 * t + 1]) * mask2[at])

    partial = [jnp.concatenate(x, axis=0) for x in sums]
    high = [x.astype(BF16) for x in partial]
    rest = [(x - h.astype(F32)).astype(BF16) for x, h in zip(partial, high)]
    p_out[...] = across(unpack, jnp.concatenate(high + rest, axis=0))
    exchange(2, lambda sec, d: p_out.at[sec * groups + d], p_in)
    sent(0, req_in)
    sent(1, f_in)
    arrive(2, p_in)
    arrived_ref[...] = p_in[...].reshape(3 * width, LANES)
    sent(2, p_in)


def finish(vel_in, place_in, arrived_in, vel_out, mom_out, mom_v, sem):
    rows = mom_out.shape[0]
    save = pltpu.make_async_copy(vel_in, vel_out, sem.at[0])
    save.start()
    both = jnp.dot(place_in[...], arrived_in[...], preferred_element_type=F32)
    for t in range(2):
        mom_v[:, t * LANES : (t + 1) * LANES] = both[t * rows : (t + 1) * rows]
    store = pltpu.make_async_copy(mom_v, mom_out, sem.at[1])
    store.start()
    save.wait()
    store.wait()


def local(ncols, grid_fields, brick_slot, block_brick, node_mask, counts, shape_t, part_mass, part_vel):
    groups = lax.axis_size("grp")
    blocks = block_brick.shape[0]
    rows = grid_fields.shape[0]
    needed = max(2, (blocks - 2 + groups - 1) // groups)
    slots = 4
    while slots < needed:
        slots *= 2
    width = groups * PIECES * slots
    vmem = pl.BlockSpec(memory_space=pltpu.VMEM)
    hbm = pl.BlockSpec(memory_space=pltpu.HBM)
    message = (3 * groups, PIECES * slots, LANES)
    vel, place, arrived = pl.pallas_call(
        functools.partial(kernel, ncols, groups, slots),
        out_shape=(
            jax.ShapeDtypeStruct((3, blocks, PBLK), F32),
            jax.ShapeDtypeStruct((2 * rows, 3 * width), BF16),
            jax.ShapeDtypeStruct((3 * width, LANES), BF16),
        ),
        in_specs=[hbm] * 8,
        out_specs=(vmem, vmem, vmem),
        scratch_shapes=[
            pltpu.VMEM((1, blocks), jnp.int32),
            pltpu.VMEM((1, brick_slot.shape[0]), jnp.int32),
            pltpu.VMEM((1, blocks), jnp.int32),
            pltpu.VMEM(grid_fields.shape, BF16),
            pltpu.VMEM(node_mask.shape, jnp.int32),
            pltpu.VMEM(part_mass.shape, F32),
            pltpu.VMEM((blocks * NODES, PBLK), BF16),
            pltpu.VMEM((3, blocks, PBLK), F32),
            pltpu.VMEM((groups, 1, width), F32),
            pltpu.VMEM((2, 1, width), F32),
            pltpu.VMEM((3 * groups, 1, width), F32),
            pltpu.VMEM(message, BF16),
            pltpu.VMEM(message, BF16),
            pltpu.VMEM(message, BF16),
            pltpu.VMEM(message, BF16),
            pltpu.SemaphoreType.DMA((8,)),
            pltpu.SemaphoreType.DMA((3,)),
            pltpu.SemaphoreType.DMA((3, 3)),
            pltpu.SemaphoreType.DMA((3, 3)),
        ],
        compiler_params=pltpu.CompilerParams(
            collective_id=0, has_side_effects=True
        ),
    )(
        block_brick.reshape(1, -1),
        brick_slot.reshape(1, -1),
        counts.reshape(1, -1),
        grid_fields,
        node_mask,
        part_mass,
        shape_t.reshape(blocks * NODES, PBLK),
        part_vel.transpose(1, 0, 2),
    )
    vel, momentum = pl.pallas_call(
        finish,
        out_shape=(
            jax.ShapeDtypeStruct((3, blocks, PBLK), F32),
            jax.ShapeDtypeStruct((rows, OUTF * NODES), F32),
        ),
        in_specs=[vmem] * 3,
        out_specs=(hbm, hbm),
        scratch_shapes=[
            pltpu.VMEM((rows, OUTF * NODES), F32),
            pltpu.SemaphoreType.DMA((2,)),
        ],
    )(vel, place, arrived)
    return vel.transpose(1, 0, 2), momentum


def solution(mesh):
    placed = (
        P(("col", "grp"), None),
        P("col"),
        P(("col", "grp")),
        P(("col", "grp"), None),
        P(("col", "grp")),
        P(("col", "grp"), None, None),
        P(("col", "grp"), None),
        P(("col", "grp"), None, None),
    )
    return jax.shard_map(
        functools.partial(local, mesh.shape["col"]),
        mesh=mesh,
        in_specs=placed,
        out_specs=(P(("col", "grp"), None, None), P(("col", "grp"), None)),
        check_vma=False,
    )
```

```python
import functools

import jax
import jax.numpy as jnp
from jax import lax
from jax.experimental import pallas as pl
from jax.experimental.pallas import tpu as pltpu
from jax.sharding import PartitionSpec as P

NODES = 64
FIELDS = 8
OUTF = 4
PBLK = 128
RIM = 16
LANES = 128
PIECES = 4
MESH = pl.DeviceIdType.MESH
F32 = jnp.float32
BF16 = jnp.bfloat16


def iota(shape, dim):
    return lax.broadcasted_iota(jnp.int32, shape, dim)


def kernel(
    ncols, groups, slots,
    bb_in, slot_in, cnt_in, grid_in, mask_in, mass_in, w_in, pv_in,
    vel_ref, mom_ref,
    bb_ref, slot_ref, cnt_ref, grid_v, mask_v, mass_v, w_v, pv_v,
    req_out, edge_out, req_in, f_out, f_in, p_out, p_in,
    in_sem, self_sem, send_sem, recv_sem,
):
    blocks = bb_ref.shape[1]
    columns = slot_ref.shape[1]
    rows = grid_in.shape[0]
    width = groups * PIECES * slots
    c = lax.axis_index("col")
    g = lax.axis_index("grp")
    has = (c > 0, None, c < ncols - 1)

    barrier = pltpu.get_barrier_semaphore()

    def peers(body_own, body_left, body_right):
        upper = g >= groups // 2
        first, way = jnp.where(upper, 0, groups - 1), jnp.where(upper, 1, -1)
        self_at = (g - first) * way
        half = groups // 2

        def own(i, carry):
            body_own(first + way * jnp.where(i >= self_at, i + 1, i))
            return carry

        def side(body, start, stop):
            def run(i, carry):
                body(first + way * i)
                return carry
            lax.fori_loop(start, stop, run, 0, unroll=groups <= 8)

        lax.fori_loop(0, half, own, 0, unroll=groups <= 8)
        pl.when(has[0])(lambda: side(body_left, 0, half))
        pl.when(has[2])(lambda: side(body_right, 0, half))
        lax.fori_loop(half, groups - 1, own, 0, unroll=groups <= 8)
        pl.when(has[0])(lambda: side(body_left, half, groups))
        pl.when(has[2])(lambda: side(body_right, half, groups))

    def greet(dc):
        def go(d):
            pl.semaphore_signal(barrier, inc=1, device_id=(c + dc, d), device_id_type=MESH)
        return go

    loads = [
        pltpu.make_async_copy(src, dst, in_sem.at[i])
        for i, (src, dst) in enumerate(
            (
                (grid_in, grid_v), (mask_in, mask_v), (mass_in, mass_v), (pv_in, pv_v), (w_in, w_v),
                (bb_in, bb_ref), (slot_in, slot_ref), (cnt_in, cnt_ref),
            )
        )
    ]
    for i in (5, 6, 7, 0, 1, 4, 2, 3):
        loads[i].start()
    peers(greet(0), greet(-1), greet(1))
    loads[5].wait()
    loads[6].wait()

    bb = bb_ref[...].astype(F32)
    slotf = slot_ref[...].astype(F32)
    eye = iota((blocks, blocks), 0) == iota((blocks, blocks), 1)

    def to_col(row):
        return jnp.sum(jnp.where(eye, row, 0.0), axis=1, keepdims=True)

    bb_col = to_col(bb)
    own_col = bb_col.astype(jnp.int32) - RIM
    is_own = (own_col >= 0) & (own_col < columns)
    hit = iota((blocks, columns), 1) == own_col
    slot_col = jnp.sum(jnp.where(hit, slotf, 0.0), axis=1, keepdims=True).astype(jnp.int32)
    owner = jnp.where(is_own, lax.div(slot_col, rows), -1)
    row_at = slot_col - owner * rows
    owner_row = jnp.sum(jnp.where(eye, owner.astype(F32), 0.0), axis=0, keepdims=True)
    same = (owner_row == owner.astype(F32)) & (iota((blocks, blocks), 1) < iota((blocks, blocks), 0))
    rank = jnp.sum(jnp.where(same, 1.0, 0.0), axis=1, keepdims=True).astype(jnp.int32)
    dest = jnp.where(is_own, owner * slots + rank, -1)
    ask = jnp.where(is_own, row_at + 1, 0).astype(F32)

    lane = iota((1, width), 1)
    lane_r = lane & (slots - 1)
    lane_j = lax.div(lane, slots) & (PIECES - 1)
    lane_g = lax.div(lane, slots * PIECES)
    from_me = lane_g == g

    def write_request(d, carry):
        match = dest == d * slots + lane_r
        values = jnp.sum(jnp.where(match, ask, 0.0), axis=0, keepdims=True)
        req_out[d] = jnp.where(from_me, values, 0.0)
        return carry

    lax.fori_loop(0, groups, write_request, 0, unroll=groups <= 8)
    first = from_me & (lane_r == 0)
    edge_out[0] = jnp.where(first, bb[:, 0:1] + 1.0, 0.0)
    edge_out[1] = jnp.where(first, bb[:, 1:2] - (columns + RIM) + 1.0, 0.0)

    def exchange(phase, out_of, into):
        def send(sec):
            def go(d):
                pltpu.make_async_remote_copy(
                    src_ref=out_of(sec, d),
                    dst_ref=into.at[(2 - sec) * groups + g],
                    send_sem=send_sem.at[phase, sec],
                    recv_sem=recv_sem.at[phase, 2 - sec],
                    device_id=(c + sec - 1, d),
                    device_id_type=MESH,
                ).start()
            return go

        peers(send(1), send(0), send(2))
        pltpu.make_async_copy(out_of(1, g), into.at[groups + g], self_sem.at[phase]).start()

    def bytes_wait(ref, start, count, sem):
        part = ref.at[pl.ds(start, count)]
        pltpu.make_async_copy(part, part, sem).wait()

    def arrive(phase, into):
        bytes_wait(into, groups, 1, self_sem.at[phase])
        bytes_wait(into, groups, groups - 1, recv_sem.at[phase, 1])
        for sec in (0, 2):
            pl.when(has[sec])(
                lambda sec=sec: bytes_wait(into, sec * groups, groups, recv_sem.at[phase, sec])
            )

    def sent(phase, into):
        bytes_wait(into, groups, groups - 1, send_sem.at[phase, 1])
        for sec in (0, 2):
            pl.when(has[sec])(
                lambda sec=sec: bytes_wait(into, sec * groups, groups, send_sem.at[phase, sec])
            )

    def clear(sec):
        for ref in (req_in, f_in, p_in):
            part = ref.at[pl.ds(sec * groups, groups)]
            part[...] = jnp.zeros(part.shape, ref.dtype)

    for sec in (0, 2):
        pl.when(jnp.logical_not(has[sec]))(lambda sec=sec: clear(sec))

    count = groups - 1 + jnp.where(has[0], groups, 0) + jnp.where(has[2], groups, 0)
    pl.semaphore_wait(barrier, count)
    exchange(
        0,
        lambda sec, d: req_out.at[d] if sec == 1 else edge_out.at[sec // 2],
        req_in,
    )

    ls = lane_g * slots + lane_r
    mine = jnp.where(dest == ls, 1.0, 0.0)
    zero_slot = lane_r == 0
    sub = iota((blocks, width), 0)
    from_left = jnp.where((sub == 0) & zero_slot, 1.0, 0.0)
    from_right = jnp.where((sub == 1) & zero_slot, 1.0, 0.0)
    wide = jnp.concatenate([from_left, mine, from_right], axis=1)
    wide_j = jnp.concatenate([lane_j] * 3, axis=1)
    unpack = jnp.concatenate(
        [jnp.where(wide_j == j, wide, 0.0) for j in range(PIECES)], axis=0
    ).astype(BF16)

    edge_lane = iota((RIM, columns), 1)
    edge_sub = iota((RIM, columns), 0)
    edge_low = jnp.sum(jnp.where(edge_lane == edge_sub, slotf, 0.0), axis=1, keepdims=True)
    edge_high = jnp.sum(
        jnp.where(edge_lane == edge_sub + (columns - RIM), slotf, 0.0), axis=1, keepdims=True
    )
    loads[7].wait()
    cnt_col = to_col(cnt_ref[...].astype(F32))
    loads[0].wait()
    grid = grid_v[...]
    grid_stack = jnp.concatenate(
        [grid[:, j * LANES : (j + 1) * LANES] for j in range(PIECES)], axis=0
    )
    loads[1].wait()
    mask = mask_v[...].astype(F32)
    mask2 = jnp.concatenate([mask, mask], axis=1)
    half = iota((1, LANES), 1) >= NODES
    low = jnp.logical_not(half)

    arrive(0, req_in)

    def asked(sec):
        total = req_in[sec * groups]
        for i in range(1, groups):
            total = total + req_in[sec * groups + i]
        return total - 1.0

    def edge_rows(value, table):
        match = iota((RIM, width), 0).astype(F32) == value
        found = jnp.sum(jnp.where(match, table + 1.0, 0.0), axis=0, keepdims=True)
        return found - 1.0 - (g * rows).astype(F32)

    want = jnp.concatenate(
        [edge_rows(asked(0), edge_low), asked(1), edge_rows(asked(2), edge_high)], axis=1
    )
    give = jnp.where(iota((rows, 3 * width), 0).astype(F32) == want, 1.0, 0.0)
    pieces = [jnp.where(wide_j == j, give, 0.0) for j in range(PIECES)]
    pack = jnp.concatenate(pieces, axis=0).astype(BF16)

    def across(matrix, stack):
        return lax.dot_general(
            matrix, stack, (((0,), (0,)), ((), ())), preferred_element_type=F32
        ).astype(BF16).reshape(3 * groups, PIECES * slots, LANES)

    f_out[...] = across(pack, grid_stack)
    exchange(1, lambda sec, d: f_out.at[sec * groups + d], f_in)

    place = jnp.concatenate(
        [pieces[t] + pieces[t + 2] for t in range(2)], axis=0
    ).astype(BF16)
    loads[2].wait()
    loads[3].wait()
    loads[4].wait()
    arrive(1, f_in)

    fields = jnp.dot(
        unpack, f_in[...].reshape(3 * width, LANES), preferred_element_type=F32
    )
    tiles = []
    for j in range(PIECES):
        v = fields[j * blocks : (j + 1) * blocks]
        r = pltpu.roll(v, NODES, 1)
        tiles.append(jnp.where(low, v, r) * mask2)
        tiles.append(jnp.where(low, r, v) * mask2)

    step = 8
    local = iota((step, LANES), 0)
    diag = [local == 2 * t + half.astype(jnp.int32) for t in range(step // 2)]
    sums = [[], []]
    plane = iota((step, PBLK), 1).astype(F32)
    for s in range(blocks // step):
        at = slice(s * step, (s + 1) * step)
        lhs = jnp.concatenate(
            [
                jnp.concatenate([jnp.where(d, tile[at], 0.0) for d in diag], axis=1)
                for tile in tiles
            ],
            axis=0,
        ).astype(BF16)
        w = w_v[pl.ds(s * step * NODES, step * NODES), :]
        interp = jnp.dot(lhs, w, preferred_element_type=F32)
        f = [interp[i * step : (i + 1) * step] for i in range(FIELDS)]
        live = jnp.where(plane < cnt_col[at], 1.0, 0.0)
        mass = mass_v[at, :]
        scale = live / (1.0 + 0.5 * f[7] * f[7])
        contrib = [mass * (1.0 + 0.5 * jnp.tanh(f[6])) * live]
        for k in range(3):
            vel = (0.4 * f[k] + 0.6 * (pv_v[k, at, :] + f[3 + k])) * scale
            vel_ref[k, at, :] = vel
            contrib.append(mass * vel)
        back = lax.dot_general(
            jnp.concatenate(contrib, axis=0).astype(BF16),
            w,
            (((1,), (1,)), ((), ())),
            preferred_element_type=F32,
        )
        folded = []
        for k in range(OUTF):
            o = back[k * step : (k + 1) * step]
            a = jnp.where(diag[0], o[:, :LANES], 0.0)
            for t in range(1, step // 2):
                a = a + jnp.where(diag[t], o[:, t * LANES : (t + 1) * LANES], 0.0)
            folded.append(a + pltpu.roll(a, NODES, 1))
        for t in range(2):
            sums[t].append(jnp.where(low, folded[2 * t], folded[2 * t + 1]) * mask2[at])

    partial = [jnp.concatenate(x, axis=0) for x in sums]
    high = [x.astype(BF16) for x in partial]
    rest = [(x - h.astype(F32)).astype(BF16) for x, h in zip(partial, high)]
    p_out[...] = across(unpack, jnp.concatenate(high + rest, axis=0))
    exchange(2, lambda sec, d: p_out.at[sec * groups + d], p_in)
    sent(0, req_in)
    sent(1, f_in)
    arrive(2, p_in)
    both = jnp.dot(place, p_in[...].reshape(3 * width, LANES), preferred_element_type=F32)
    for t in range(2):
        mom_ref[:, t * LANES : (t + 1) * LANES] = both[t * rows : (t + 1) * rows]
    sent(2, p_in)


def finish(vel_in, mom_in, vel_out, mom_out, sem):
    saves = [
        pltpu.make_async_copy(src, dst, sem.at[i])
        for i, (src, dst) in enumerate(((vel_in, vel_out), (mom_in, mom_out)))
    ]
    for save in saves:
        save.start()
    for save in saves:
        save.wait()


def local(ncols, grid_fields, brick_slot, block_brick, node_mask, counts, shape_t, part_mass, part_vel):
    groups = lax.axis_size("grp")
    blocks = block_brick.shape[0]
    rows = grid_fields.shape[0]
    needed = max(2, (blocks - 2 + groups - 1) // groups)
    slots = 4
    while slots < needed:
        slots *= 2
    width = groups * PIECES * slots
    vmem = pl.BlockSpec(memory_space=pltpu.VMEM)
    hbm = pl.BlockSpec(memory_space=pltpu.HBM)
    message = (3 * groups, PIECES * slots, LANES)
    vel, momentum = pl.pallas_call(
        functools.partial(kernel, ncols, groups, slots),
        out_shape=(
            pltpu.VMEM((3, blocks, PBLK), F32),
            pltpu.VMEM((rows, OUTF * NODES), F32),
        ),
        in_specs=[hbm] * 8,
        out_specs=(vmem, vmem),
        scratch_shapes=[
            pltpu.VMEM((1, blocks), jnp.int32),
            pltpu.VMEM((1, brick_slot.shape[0]), jnp.int32),
            pltpu.VMEM((1, blocks), jnp.int32),
            pltpu.VMEM(grid_fields.shape, BF16),
            pltpu.VMEM(node_mask.shape, jnp.int32),
            pltpu.VMEM(part_mass.shape, F32),
            pltpu.VMEM((blocks * NODES, PBLK), BF16),
            pltpu.VMEM((3, blocks, PBLK), F32),
            pltpu.VMEM((groups, 1, width), F32),
            pltpu.VMEM((2, 1, width), F32),
            pltpu.VMEM((3 * groups, 1, width), F32),
            pltpu.VMEM(message, BF16),
            pltpu.VMEM(message, BF16),
            pltpu.VMEM(message, BF16),
            pltpu.VMEM(message, BF16),
            pltpu.SemaphoreType.DMA((8,)),
            pltpu.SemaphoreType.DMA((3,)),
            pltpu.SemaphoreType.DMA((3, 3)),
            pltpu.SemaphoreType.DMA((3, 3)),
        ],
        compiler_params=pltpu.CompilerParams(
            collective_id=0, has_side_effects=True, vmem_limit_bytes=32 * 1024 * 1024
        ),
    )(
        *(
            pltpu.with_memory_space_constraint(x, pltpu.HBM)
            for x in (
                block_brick.reshape(1, -1),
                brick_slot.reshape(1, -1),
                counts.reshape(1, -1),
                grid_fields,
                node_mask,
                part_mass,
                shape_t.reshape(blocks * NODES, PBLK),
                part_vel.transpose(1, 0, 2),
            )
        )
    )
    vel, momentum = pl.pallas_call(
        finish,
        out_shape=(
            pltpu.HBM((3, blocks, PBLK), F32),
            pltpu.HBM((rows, OUTF * NODES), F32),
        ),
        in_specs=[vmem] * 2,
        out_specs=(hbm, hbm),
        scratch_shapes=[pltpu.SemaphoreType.DMA((2,))],
    )(
        pltpu.with_memory_space_constraint(vel, pltpu.VMEM),
        pltpu.with_memory_space_constraint(momentum, pltpu.VMEM),
    )
    return vel.transpose(1, 0, 2), momentum


def solution(mesh):
    placed = (
        P(("col", "grp"), None),
        P("col"),
        P(("col", "grp")),
        P(("col", "grp"), None),
        P(("col", "grp")),
        P(("col", "grp"), None, None),
        P(("col", "grp"), None),
        P(("col", "grp"), None, None),
    )
    return jax.shard_map(
        functools.partial(local, mesh.shape["col"]),
        mesh=mesh,
        in_specs=placed,
        out_specs=(P(("col", "grp"), None, None), P(("col", "grp"), None)),
        check_vma=False,
    )
```

```python
import functools

import jax
import jax.numpy as jnp
from jax import lax
from jax.experimental import pallas as pl
from jax.experimental.pallas import tpu as pltpu
from jax.sharding import PartitionSpec as P

NODES = 64
FIELDS = 8
OUTF = 4
PBLK = 128
RIM = 16
LANES = 128
PIECES = 4
MESH = pl.DeviceIdType.MESH
F32 = jnp.float32
BF16 = jnp.bfloat16


def iota(shape, dim):
    return lax.broadcasted_iota(jnp.int32, shape, dim)


def kernel(
    ncols, groups, slots,
    bb_in, slot_in, cnt_in, grid_in, mask_in, mass_in, w_in, pv_in,
    vel_ref, mom_ref,
    bb_ref, slot_ref, cnt_ref, grid_v, mask_v, mass_v, w_v, pv_v,
    req_out, edge_out, req_in, f_out, f_in, p_out, p_in, e_out, e_in,
    in_sem, self_sem, send_sem, recv_sem,
):
    blocks = bb_ref.shape[1]
    columns = slot_ref.shape[1]
    rows = grid_in.shape[0]
    width = groups * PIECES * slots
    c = lax.axis_index("col")
    g = lax.axis_index("grp")
    has = (c > 0, None, c < ncols - 1)

    barrier = pltpu.get_barrier_semaphore()

    def peers(body_own, body_left, body_right):
        upper = g >= groups // 2
        first, way = jnp.where(upper, 0, groups - 1), jnp.where(upper, 1, -1)
        self_at = (g - first) * way
        half = groups // 2

        def own(i, carry):
            body_own(first + way * jnp.where(i >= self_at, i + 1, i))
            return carry

        def side(body, start, stop):
            def run(i, carry):
                body(first + way * i)
                return carry
            lax.fori_loop(start, stop, run, 0, unroll=groups <= 8)

        lax.fori_loop(0, half, own, 0, unroll=groups <= 8)
        pl.when(has[0])(lambda: side(body_left, 0, half))
        pl.when(has[2])(lambda: side(body_right, 0, half))
        lax.fori_loop(half, groups - 1, own, 0, unroll=groups <= 8)
        pl.when(has[0])(lambda: side(body_left, half, groups))
        pl.when(has[2])(lambda: side(body_right, half, groups))

    def greet(dc):
        def go(d):
            pl.semaphore_signal(barrier, inc=1, device_id=(c + dc, d), device_id_type=MESH)
        return go

    loads = [
        pltpu.make_async_copy(src, dst, in_sem.at[i])
        for i, (src, dst) in enumerate(
            (
                (grid_in, grid_v), (mask_in, mask_v), (mass_in, mass_v), (pv_in, pv_v), (w_in, w_v),
                (bb_in, bb_ref), (slot_in, slot_ref), (cnt_in, cnt_ref),
            )
        )
    ]
    for i in (5, 6, 7, 0, 1, 4, 2, 3):
        loads[i].start()
    peers(greet(0), greet(-1), greet(1))
    loads[5].wait()
    loads[6].wait()

    bb = bb_ref[...].astype(F32)
    slotf = slot_ref[...].astype(F32)
    eye = iota((blocks, blocks), 0) == iota((blocks, blocks), 1)

    def to_col(row):
        return jnp.sum(jnp.where(eye, row, 0.0), axis=1, keepdims=True)

    bb_col = to_col(bb)
    own_col = bb_col.astype(jnp.int32) - RIM
    is_own = (own_col >= 0) & (own_col < columns)
    hit = iota((blocks, columns), 1) == own_col
    slot_col = jnp.sum(jnp.where(hit, slotf, 0.0), axis=1, keepdims=True).astype(jnp.int32)
    owner = jnp.where(is_own, lax.div(slot_col, rows), -1)
    row_at = slot_col - owner * rows
    owner_row = jnp.sum(jnp.where(eye, owner.astype(F32), 0.0), axis=0, keepdims=True)
    same = (owner_row == owner.astype(F32)) & (iota((blocks, blocks), 1) < iota((blocks, blocks), 0))
    rank = jnp.sum(jnp.where(same, 1.0, 0.0), axis=1, keepdims=True).astype(jnp.int32)
    dest = jnp.where(is_own, owner * slots + rank, -1)
    ask = jnp.where(is_own, row_at + 1, 0).astype(F32)

    lane = iota((1, width), 1)
    lane_r = lane & (slots - 1)
    lane_j = lax.div(lane, slots) & (PIECES - 1)
    lane_g = lax.div(lane, slots * PIECES)
    from_me = lane_g == g

    def write_request(d, carry):
        match = dest == d * slots + lane_r
        values = jnp.sum(jnp.where(match, ask, 0.0), axis=0, keepdims=True)
        req_out[d] = jnp.where(from_me, values, 0.0)
        return carry

    lax.fori_loop(0, groups, write_request, 0, unroll=groups <= 8)
    first = from_me & (lane_r == 0)
    edge_out[0] = jnp.where(first, bb[:, 0:1] + 1.0, 0.0)
    edge_out[1] = jnp.where(first, bb[:, 1:2] - (columns + RIM) + 1.0, 0.0)

    def exchange(phase, out_of, into):
        def send(sec):
            def go(d):
                pltpu.make_async_remote_copy(
                    src_ref=out_of(sec, d),
                    dst_ref=into.at[(2 - sec) * groups + g],
                    send_sem=send_sem.at[phase, sec],
                    recv_sem=recv_sem.at[phase, 2 - sec],
                    device_id=(c + sec - 1, d),
                    device_id_type=MESH,
                ).start()
            return go

        peers(send(1), send(0), send(2))
        pltpu.make_async_copy(out_of(1, g), into.at[groups + g], self_sem.at[phase]).start()

    def bytes_wait(ref, start, count, sem):
        part = ref.at[pl.ds(start, count)]
        pltpu.make_async_copy(part, part, sem).wait()

    def arrive(phase, into):
        bytes_wait(into, groups, 1, self_sem.at[phase])
        bytes_wait(into, groups, groups - 1, recv_sem.at[phase, 1])
        for sec in (0, 2):
            pl.when(has[sec])(
                lambda sec=sec: bytes_wait(into, sec * groups, groups, recv_sem.at[phase, sec])
            )

    def sent(phase, into):
        bytes_wait(into, groups, groups - 1, send_sem.at[phase, 1])
        for sec in (0, 2):
            pl.when(has[sec])(
                lambda sec=sec: bytes_wait(into, sec * groups, groups, send_sem.at[phase, sec])
            )

    def clear(sec):
        for ref, at in ((req_in, sec), (f_in, sec), (e_in, sec // 2)):
            part = ref.at[pl.ds(at * groups, groups)]
            part[...] = jnp.zeros(part.shape, ref.dtype)

    for sec in (0, 2):
        pl.when(jnp.logical_not(has[sec]))(lambda sec=sec: clear(sec))

    count = groups - 1 + jnp.where(has[0], groups, 0) + jnp.where(has[2], groups, 0)
    pl.semaphore_wait(barrier, count)
    exchange(
        0,
        lambda sec, d: req_out.at[d] if sec == 1 else edge_out.at[sec // 2],
        req_in,
    )

    ls = lane_g * slots + lane_r
    mine = jnp.where(dest == ls, 1.0, 0.0)
    zero_slot = lane_r == 0
    sub = iota((blocks, width), 0)
    from_left = jnp.where((sub == 0) & zero_slot, 1.0, 0.0)
    from_right = jnp.where((sub == 1) & zero_slot, 1.0, 0.0)
    wide = jnp.concatenate([from_left, mine, from_right], axis=1)
    wide_j = jnp.concatenate([lane_j] * 3, axis=1)
    unpack = jnp.concatenate(
        [jnp.where(wide_j == j, wide, 0.0) for j in range(PIECES)], axis=0
    ).astype(BF16)

    edge_lane = iota((RIM, columns), 1)
    edge_sub = iota((RIM, columns), 0)
    edge_low = jnp.sum(jnp.where(edge_lane == edge_sub, slotf, 0.0), axis=1, keepdims=True)
    edge_high = jnp.sum(
        jnp.where(edge_lane == edge_sub + (columns - RIM), slotf, 0.0), axis=1, keepdims=True
    )
    loads[7].wait()
    cnt_col = to_col(cnt_ref[...].astype(F32))
    loads[0].wait()
    grid = grid_v[...]
    grid_stack = jnp.concatenate(
        [grid[:, j * LANES : (j + 1) * LANES] for j in range(PIECES)], axis=0
    )
    loads[1].wait()
    mask = mask_v[...].astype(F32)
    mask2 = jnp.concatenate([mask, mask], axis=1)
    half = iota((1, LANES), 1) >= NODES
    low = jnp.logical_not(half)

    arrive(0, req_in)

    def asked(sec):
        total = req_in[sec * groups]
        for i in range(1, groups):
            total = total + req_in[sec * groups + i]
        return total - 1.0

    def edge_rows(value, table):
        match = iota((RIM, width), 0).astype(F32) == value
        found = jnp.sum(jnp.where(match, table + 1.0, 0.0), axis=0, keepdims=True)
        return found - 1.0 - (g * rows).astype(F32)

    want = jnp.concatenate(
        [edge_rows(asked(0), edge_low), asked(1), edge_rows(asked(2), edge_high)], axis=1
    )
    give = jnp.where(iota((rows, 3 * width), 0).astype(F32) == want, 1.0, 0.0)
    pieces = [jnp.where(wide_j == j, give, 0.0) for j in range(PIECES)]
    pack = jnp.concatenate(pieces, axis=0).astype(BF16)

    def across(matrix, stack):
        return lax.dot_general(
            matrix, stack, (((0,), (0,)), ((), ())), preferred_element_type=F32
        ).astype(BF16).reshape(3 * groups, PIECES * slots, LANES)

    f_out[...] = across(pack, grid_stack)
    exchange(1, lambda sec, d: f_out.at[sec * groups + d], f_in)

    place = jnp.concatenate(
        [pieces[t] + pieces[t + 2] for t in range(2)], axis=0
    ).astype(BF16)
    loads[2].wait()
    loads[3].wait()
    loads[4].wait()
    arrive(1, f_in)

    fields = jnp.dot(
        unpack, f_in[...].reshape(3 * width, LANES), preferred_element_type=F32
    )
    tiles = []
    for j in range(PIECES):
        v = fields[j * blocks : (j + 1) * blocks]
        r = pltpu.roll(v, NODES, 1)
        tiles.append(jnp.where(low, v, r) * mask2)
        tiles.append(jnp.where(low, r, v) * mask2)

    step = 8
    local = iota((step, LANES), 0)
    diag = [local == 2 * t + half.astype(jnp.int32) for t in range(step // 2)]
    sums = [[], []]
    plane = iota((step, PBLK), 1).astype(F32)
    for s in range(blocks // step):
        at = slice(s * step, (s + 1) * step)
        lhs = jnp.concatenate(
            [
                jnp.concatenate([jnp.where(d, tile[at], 0.0) for d in diag], axis=1)
                for tile in tiles
            ],
            axis=0,
        ).astype(BF16)
        w = w_v[pl.ds(s * step * NODES, step * NODES), :]
        interp = jnp.dot(lhs, w, preferred_element_type=F32)
        f = [interp[i * step : (i + 1) * step] for i in range(FIELDS)]
        live = jnp.where(plane < cnt_col[at], 1.0, 0.0)
        mass = mass_v[at, :]
        scale = live / (1.0 + 0.5 * f[7] * f[7])
        contrib = [mass * (1.0 + 0.5 * jnp.tanh(f[6])) * live]
        for k in range(3):
            vel = (0.4 * f[k] + 0.6 * (pv_v[k, at, :] + f[3 + k])) * scale
            vel_ref[k, at, :] = vel
            contrib.append(mass * vel)
        back = lax.dot_general(
            jnp.concatenate(contrib, axis=0).astype(BF16),
            w,
            (((1,), (1,)), ((), ())),
            preferred_element_type=F32,
        )
        folded = []
        for k in range(OUTF):
            o = back[k * step : (k + 1) * step]
            a = jnp.where(diag[0], o[:, :LANES], 0.0)
            for t in range(1, step // 2):
                a = a + jnp.where(diag[t], o[:, t * LANES : (t + 1) * LANES], 0.0)
            folded.append(a + pltpu.roll(a, NODES, 1))
        for t in range(2):
            sums[t].append(jnp.where(low, folded[2 * t], folded[2 * t + 1]) * mask2[at])

    partial = [jnp.concatenate(x, axis=0) for x in sums]
    high = [x.astype(BF16) for x in partial]
    rest = [(x - h.astype(F32)).astype(BF16) for x, h in zip(partial, high)]
    p_out[...] = across(unpack, jnp.concatenate(high + rest, axis=0))
    for i in range(2):
        e_out[i] = jnp.concatenate([x[i : i + 1] for x in partial], axis=1)

    def deliver(sec):
        def go(d):
            pltpu.make_async_remote_copy(
                src_ref=p_out.at[groups + d] if sec == 1 else e_out.at[sec // 2],
                dst_ref=p_in.at[groups + g] if sec == 1 else e_in.at[(1 - sec // 2) * groups + g],
                send_sem=send_sem.at[2, sec],
                recv_sem=recv_sem.at[2, 2 - sec],
                device_id=(c + sec - 1, d),
                device_id_type=MESH,
            ).start()
        return go

    peers(deliver(1), deliver(0), deliver(2))
    pltpu.make_async_copy(p_out.at[groups + g], p_in.at[groups + g], self_sem.at[2]).start()

    def edges(sem):
        for sec in (0, 2):
            pl.when(has[sec])(
                lambda sec=sec: bytes_wait(e_in, sec // 2 * groups, groups, sem.at[2, sec])
            )

    sent(0, req_in)
    sent(1, f_in)
    bytes_wait(p_in, groups, 1, self_sem.at[2])
    bytes_wait(p_in, groups, groups - 1, recv_sem.at[2, 1])
    edges(recv_sem)
    both = jnp.dot(
        place[:, width : 2 * width],
        p_in[groups : 2 * groups].reshape(width, LANES),
        preferred_element_type=F32,
    )
    row_id = iota((rows, OUTF * NODES), 0).astype(F32)
    added = jnp.zeros((rows, OUTF * NODES), F32)
    for k in range(2 * groups):
        at = (k // groups * 2) * width + k % groups * PIECES * slots
        added = added + jnp.where(row_id == want[:, at : at + 1], e_in[k], 0.0)
    for t in range(2):
        mom_ref[:, t * LANES : (t + 1) * LANES] = (
            both[t * rows : (t + 1) * rows] + added[:, t * LANES : (t + 1) * LANES]
        )
    bytes_wait(p_in, groups, groups - 1, send_sem.at[2, 1])
    edges(send_sem)


def finish(vel_in, mom_in, vel_out, mom_out, sem):
    saves = [
        pltpu.make_async_copy(src, dst, sem.at[i])
        for i, (src, dst) in enumerate(((vel_in, vel_out), (mom_in, mom_out)))
    ]
    for save in saves:
        save.start()
    for save in saves:
        save.wait()


def local(ncols, grid_fields, brick_slot, block_brick, node_mask, counts, shape_t, part_mass, part_vel):
    groups = lax.axis_size("grp")
    blocks = block_brick.shape[0]
    rows = grid_fields.shape[0]
    needed = max(2, (blocks - 2 + groups - 1) // groups)
    slots = 4
    while slots < needed:
        slots *= 2
    width = groups * PIECES * slots
    vmem = pl.BlockSpec(memory_space=pltpu.VMEM)
    hbm = pl.BlockSpec(memory_space=pltpu.HBM)
    message = (3 * groups, PIECES * slots, LANES)
    vel, momentum = pl.pallas_call(
        functools.partial(kernel, ncols, groups, slots),
        out_shape=(
            pltpu.VMEM((3, blocks, PBLK), F32),
            pltpu.VMEM((rows, OUTF * NODES), F32),
        ),
        in_specs=[hbm] * 8,
        out_specs=(vmem, vmem),
        scratch_shapes=[
            pltpu.VMEM((1, blocks), jnp.int32),
            pltpu.VMEM((1, brick_slot.shape[0]), jnp.int32),
            pltpu.VMEM((1, blocks), jnp.int32),
            pltpu.VMEM(grid_fields.shape, BF16),
            pltpu.VMEM(node_mask.shape, jnp.int32),
            pltpu.VMEM(part_mass.shape, F32),
            pltpu.VMEM((blocks * NODES, PBLK), BF16),
            pltpu.VMEM((3, blocks, PBLK), F32),
            pltpu.VMEM((groups, 1, width), F32),
            pltpu.VMEM((2, 1, width), F32),
            pltpu.VMEM((3 * groups, 1, width), F32),
            pltpu.VMEM(message, BF16),
            pltpu.VMEM(message, BF16),
            pltpu.VMEM(message, BF16),
            pltpu.VMEM(message, BF16),
            pltpu.VMEM((2, 1, OUTF * NODES), F32),
            pltpu.VMEM((2 * groups, 1, OUTF * NODES), F32),
            pltpu.SemaphoreType.DMA((8,)),
            pltpu.SemaphoreType.DMA((3,)),
            pltpu.SemaphoreType.DMA((3, 3)),
            pltpu.SemaphoreType.DMA((3, 3)),
        ],
        compiler_params=pltpu.CompilerParams(
            collective_id=0, has_side_effects=True, vmem_limit_bytes=32 * 1024 * 1024
        ),
    )(
        *(
            pltpu.with_memory_space_constraint(x, pltpu.HBM)
            for x in (
                block_brick.reshape(1, -1),
                brick_slot.reshape(1, -1),
                counts.reshape(1, -1),
                grid_fields,
                node_mask,
                part_mass,
                shape_t.reshape(blocks * NODES, PBLK),
                part_vel.transpose(1, 0, 2),
            )
        )
    )
    vel, momentum = pl.pallas_call(
        finish,
        out_shape=(
            pltpu.HBM((3, blocks, PBLK), F32),
            pltpu.HBM((rows, OUTF * NODES), F32),
        ),
        in_specs=[vmem] * 2,
        out_specs=(hbm, hbm),
        scratch_shapes=[pltpu.SemaphoreType.DMA((2,))],
    )(
        pltpu.with_memory_space_constraint(vel, pltpu.VMEM),
        pltpu.with_memory_space_constraint(momentum, pltpu.VMEM),
    )
    return vel.transpose(1, 0, 2), momentum


def solution(mesh):
    placed = (
        P(("col", "grp"), None),
        P("col"),
        P(("col", "grp")),
        P(("col", "grp"), None),
        P(("col", "grp")),
        P(("col", "grp"), None, None),
        P(("col", "grp"), None),
        P(("col", "grp"), None, None),
    )
    return jax.shard_map(
        functools.partial(local, mesh.shape["col"]),
        mesh=mesh,
        in_specs=placed,
        out_specs=(P(("col", "grp"), None, None), P(("col", "grp"), None)),
        check_vma=False,
    )
```
